512 devices in a mesh: replica: 16 (over y_lo, z), fsdp: 32 (over x, y_hi, core).
Axes of the slice: x: 4, y: 8 (y_hi: 4, y_lo: 2; y = y_hi * 2 + y_lo), z: 8, core: 2. Of those that a mesh axis runs over, the one named last changes fastest.
Arguments:
- acts: bfloat16 [16, 6144, 2048], P('replica', 'fsdp'), may hold values from -6 to 6
- upstream: bfloat16 [16, 6144, 2048], P('replica', 'fsdp'), may hold values from -0.076171875 to 0.076171875
- inner_params: float32 [16, 32, 256, 512], P('replica', 'fsdp'), may hold values from -6 to 6
- first_moment: float32 [16, 32, 256, 512], P('replica', 'fsdp'), may hold values from -2 to 2
- second_moment: float32 [16, 32, 256, 512], P('replica', 'fsdp'), may hold values from 0.05 to 2
- anchor: float32 [32, 256, 512], P('fsdp', 'replica'), may hold values from -6 to 6
- outer_momentum: float32 [32, 256, 512], P('fsdp', 'replica'), may hold values from -3 to 3
Outputs:
- new_params: float32 [32, 256, 512], P('fsdp')
- new_momentum: float32 [32, 256, 512], P('fsdp', 'replica')
- new_first: float32 [16, 32, 256, 512], P('replica', 'fsdp')
- new_second: float32 [16, 32, 256, 512], P('replica', 'fsdp')
The draws below stay inside these ranges and needn't reach their ends.
All inputs are finite; a program needn't handle non-finite values.
Results may differ from the reference program's by a relative error of at most 0.0003.
Values may be sent and summed in bfloat16 or wider, within the bound.
No kernel may reach another device: no remote copies, remote signals or barrier semaphores. Data moves between devices by JAX's collectives and lax.ppermute only.
A program may use at most 64 MiB of HBM per device.

```python
import math
import jax
import jax.numpy as jnp
from jax import lax

IN = 2048
OUT = 2048
STEP = 500
REPLICAS = 16
BLOCKS = 32
TOKENS = 6144
BR = 256
BC = 512
N_REPLICA = 16
N_FSDP = 32


def block_scale(rng, dims, shards, smallest, top_value):
    loudness, own = 1.0, jax.random.fold_in(rng, 6)
    for axis_at, parts in shards:
        steps = jnp.exp(jax.random.uniform(jax.random.fold_in(own, axis_at), (parts,), jnp.float32, smallest / len(shards), top_value / len(shards)))
        loudness = loudness * jnp.repeat(steps, dims[axis_at] // parts).reshape([-1 if axis == axis_at else 1 for axis in range(len(dims))])
    return loudness


def noise(rng, dims, deviation, limit, shards=(), kind=jnp.bfloat16):
    entries = jax.random.normal(rng, dims, jnp.float32) * deviation
    if len(shards) > 0:
        entries = block_scale(rng, dims, shards, -0.22, 0.18) * entries
    return jnp.clip(entries, min=-limit, max=limit).astype(kind)


def setup_inputs(seed: int = 0) -> dict:
    splits = jax.random.split(jax.random.key(seed), 8)
    return {
        "acts": noise(splits[0], (REPLICAS, TOKENS, IN), 1.0, 6.0, ((0, 16), (1, 32))),
        "upstream": noise(splits[1], (REPLICAS, TOKENS, OUT), (TOKENS ** -0.5), 0.076171875, ((0, 16), (1, 32))),
        "inner_params": noise(splits[2], (REPLICAS, BLOCKS, BR, BC), 1.0, 6.0, ((0, 16), (1, 32)), jnp.float32),
        "first_moment": noise(splits[3], (REPLICAS, BLOCKS, BR, BC), 0.3, 2.0, ((0, 16), (1, 32)), jnp.float32),
        "second_moment": jnp.clip(jnp.exp(math.log(2.0) - 3.6888794 * jax.random.uniform(splits[4], (REPLICAS, BLOCKS, BR, BC), jnp.float32) ** block_scale(splits[4], (REPLICAS, BLOCKS, BR, BC), ((0, 16), (1, 32)), -0.2, 0.2)), 0.05, 2.0),
        "anchor": noise(splits[5], (BLOCKS, BR, BC), 1.0, 6.0, ((0, 32), (1, 16)), jnp.float32),
        "outer_momentum": noise(splits[6], (BLOCKS, BR, BC), 0.5, 3.0, ((0, 32), (1, 16)), jnp.float32),
    }


beta_one = 0.9
beta_two = 0.95
adam_eps = 1e-08
decay_rate = 0.1
inner_rate = 0.02
outer_rate = 0.7
outer_mu = 0.9

def to_blocks(full):
    rows = full.reshape(N_FSDP // 4, BR, 4, BC)
    return rows.transpose(0, 2, 1, 3).reshape(N_FSDP, BR, BC)

def reference(acts, upstream, inner_params, first_moment, second_moment, anchor, outer_momentum):
    fix_one = 1.0 - beta_one ** STEP
    fix_two = 1.0 - beta_two ** STEP

    def replica_step(packed):
        tokens, grads_out, params, moment_one, moment_two = packed
        gradient = to_blocks(jnp.dot(tokens.T, grads_out, preferred_element_type=jnp.float32))
        moment_one = beta_one * moment_one + (1.0 - beta_one) * gradient
        moment_two = beta_two * moment_two + (1.0 - beta_two) * gradient * gradient
        update = moment_one / fix_one / (jnp.sqrt(moment_two / fix_two) + adam_eps) + decay_rate * params
        return (params - inner_rate * update, moment_one, moment_two)
    stepped, new_first, new_second = lax.map(replica_step, (acts, upstream, inner_params, first_moment, second_moment))
    pseudo = anchor - lax.optimization_barrier(jnp.sum(stepped, axis=0)) / N_REPLICA
    new_momentum = outer_mu * outer_momentum + pseudo
    new_params = anchor - outer_rate * (pseudo + outer_mu * new_momentum)
    return (new_params, new_momentum, new_first, new_second)
```

```python
import jax
import jax.numpy as jnp
from jax import lax
from jax.sharding import PartitionSpec as P

STEP = 500


beta_one = 0.9
beta_two = 0.95
adam_eps = 1e-08
decay_rate = 0.1
inner_rate = 0.02
outer_rate = 0.7
outer_mu = 0.9

SIDE = 4
SHARDS = 32


def ring_partner(i, stage):
    return i ^ 1 if stage == 0 else i ^ 3


def place(i):
    return i // 8, i // 2 % SIDE, i % 2


def core_pairs():
    return [(i, i ^ 1) for i in range(SHARDS)]


def x_pairs(stage):
    pairs = []
    for i in range(SHARDS):
        x, y, c = place(i)
        pairs.append((i, ring_partner(x, stage ^ c) * 8 + y * 2 + c))
    return pairs


def y_pairs(stage):
    pairs = []
    for i in range(SHARDS):
        x, y, c = place(i)
        pairs.append((i, x * 8 + ring_partner(y, stage ^ c) * 2 + c))
    return pairs


def body(acts, upstream, inner_params, first_moment, second_moment, anchor, outer_momentum):
    members = lax.axis_size("replica")
    me = lax.axis_index("fsdp")
    x, y, c = me // 8, me // 2 % SIDE, me % 2
    near, far = jnp.where(c == 0, 1, 3), jnp.where(c == 0, 3, 1)
    a = acts[0]
    u = upstream[0]
    count = a.shape[0]
    rows, cols = 256, 512

    def a_for(dest):
        return lax.dynamic_slice(a, (0, dest * 2 * rows), (count, 2 * rows))

    def u_for(core):
        return jnp.concatenate(
            [lax.dynamic_slice(u, (0, (k * 2 + core) * cols), (count, cols)) for k in range(2)], 1
        )

    a_sent = jnp.concatenate([a_for(x ^ near), a_for(x ^ 2)], 0)
    a_one = lax.ppermute(a_sent, "fsdp", x_pairs(0))
    u_other = lax.ppermute(u_for(1 - c), "fsdp", core_pairs())
    u_chip = jnp.concatenate([u_for(c), u_other], 0)
    u_one = lax.ppermute(u_chip, "fsdp", x_pairs(0))
    a_two = lax.ppermute(
        jnp.concatenate([a_for(x ^ far), a_one[count:]], 0), "fsdp", x_pairs(1)
    )
    u_half = jnp.concatenate([u_chip, u_one], 0)
    u_two = lax.ppermute(u_half, "fsdp", x_pairs(1))
    a_core = jnp.concatenate([a_for(x), a_one[:count], a_two], 0)
    a_other = lax.ppermute(a_core, "fsdp", core_pairs())
    order = [a_core[i * count : (i + 1) * count] for i in range(4)]
    other = [a_other[i * count : (i + 1) * count] for i in (0, 2, 1, 3)]
    a_all = jnp.concatenate([t for pair in zip(order, other) for t in pair], 0)
    u_all = jnp.concatenate([u_half, u_two], 0)

    def part(dest):
        left = lax.dynamic_slice(a_all, (0, dest // 2 * rows), (8 * count, rows))
        right = lax.dynamic_slice(u_all, (0, dest % 2 * cols), (8 * count, cols))
        return lax.dot_general(
            left, right, (((0,), (0,)), ((), ())), preferred_element_type=jnp.float32
        )

    g_sent = jnp.stack([part(y ^ far ^ near), part(y ^ near)])
    g_one = lax.ppermute(g_sent, "fsdp", y_pairs(0))
    g_two = lax.ppermute(part(y ^ far) + g_one[0], "fsdp", y_pairs(1))
    gradient = part(y) + g_one[1] + g_two

    fix_one = 1.0 - beta_one**STEP
    fix_two = 1.0 - beta_two**STEP
    params = inner_params[0, 0]
    moment_one = beta_one * first_moment[0, 0] + (1.0 - beta_one) * gradient
    moment_two = beta_two * second_moment[0, 0] + (1.0 - beta_two) * gradient * gradient
    update = (
        moment_one / fix_one / (jnp.sqrt(moment_two / fix_two) + adam_eps) + decay_rate * params
    )
    stepped = params - inner_rate * update

    slice_rows = rows // members
    parts = lax.all_to_all(
        stepped.reshape(members, slice_rows, cols), "replica", split_axis=0, concat_axis=0, tiled=True
    )
    pseudo = anchor[0] - jnp.sum(parts, axis=0) / members
    new_momentum = outer_mu * outer_momentum[0] + pseudo
    new_params = anchor[0] - outer_rate * (pseudo + outer_mu * new_momentum)
    gathered = lax.all_to_all(
        jnp.broadcast_to(new_params[None], (members, slice_rows, cols)),
        "replica",
        split_axis=0,
        concat_axis=0,
        tiled=True,
    ).reshape(rows, cols)
    return (gathered[None], new_momentum[None], moment_one[None, None], moment_two[None, None])


def solution(mesh):
    in_specs = (
        P("replica", "fsdp", None),
        P("replica", "fsdp", None),
        P("replica", "fsdp", None, None),
        P("replica", "fsdp", None, None),
        P("replica", "fsdp", None, None),
        P("fsdp", "replica", None),
        P("fsdp", "replica", None),
    )
    out_specs = (
        P("fsdp", None, None),
        P("fsdp", "replica", None),
        P("replica", "fsdp", None, None),
        P("replica", "fsdp", None, None),
    )
    return jax.shard_map(body, mesh=mesh, in_specs=in_specs, out_specs=out_specs, check_vma=False)
```

```python
import jax
import jax.numpy as jnp
from jax import lax
from jax.sharding import PartitionSpec as P

STEP = 500


beta_one = 0.9
beta_two = 0.95
adam_eps = 1e-08
decay_rate = 0.1
inner_rate = 0.02
outer_rate = 0.7
outer_mu = 0.9

SIDE = 4
SHARDS = 32


def ring_partner(i, stage):
    return i ^ 1 if stage == 0 else i ^ 3


def place(i):
    return i // 8, i // 2 % SIDE, i % 2


def core_pairs():
    return [(i, i ^ 1) for i in range(SHARDS)]


def x_pairs(stage):
    pairs = []
    for i in range(SHARDS):
        x, y, c = place(i)
        pairs.append((i, ring_partner(x, stage ^ c) * 8 + y * 2 + c))
    return pairs


def y_pairs(stage):
    pairs = []
    for i in range(SHARDS):
        x, y, c = place(i)
        pairs.append((i, x * 8 + ring_partner(y, stage ^ c) * 2 + c))
    return pairs


def body(acts, upstream, inner_params, first_moment, second_moment, anchor, outer_momentum):
    members = lax.axis_size("replica")
    me = lax.axis_index("fsdp")
    x, y, c = me >> 3, (me >> 1) & 3, me & 1
    near, far = jnp.where(c == 0, 1, 3), jnp.where(c == 0, 3, 1)
    a = acts[0]
    u = upstream[0]
    count = a.shape[0]
    rows, cols = 256, 512

    def a_for(dest):
        return lax.dynamic_slice(a, (0, dest * 2 * rows), (count, 2 * rows))

    def u_for(core):
        return [lax.dynamic_slice(u, (0, (k * 2 + core) * cols), (count, cols)) for k in range(2)]

    def pieces(t):
        return [t[i * count : (i + 1) * count] for i in range(t.shape[0] // count)]

    u_own = u_for(c)
    u_swap = lax.ppermute(jnp.concatenate(u_for(1 - c), 0), "fsdp", core_pairs())
    one = lax.ppermute(
        jnp.concatenate([a_for(x ^ near), *u_own, a_for(x ^ 2)], 0), "fsdp", x_pairs(0)
    )
    two = lax.ppermute(jnp.concatenate([a_for(x ^ far), *u_own], 0), "fsdp", x_pairs(1))
    one_swap = lax.ppermute(u_swap, "fsdp", x_pairs(0))
    two_swap = lax.ppermute(u_swap, "fsdp", x_pairs(1))
    three = lax.ppermute(one[count:], "fsdp", x_pairs(1))
    three_swap = lax.ppermute(one_swap, "fsdp", x_pairs(1))
    a_core = jnp.concatenate([a_for(x), one[:count], two[:count], three[2 * count :]], 0)
    a_other = lax.ppermute(a_core, "fsdp", core_pairs())
    other = pieces(a_other)
    a_all = jnp.concatenate([a_core, other[0], other[2], other[1], other[3]], 0)
    u_core = [u_own, pieces(one)[1:3], pieces(two)[1:], pieces(three)[:2]]
    u_rest = [pieces(u_swap), pieces(one_swap), pieces(two_swap), pieces(three_swap)]
    u_all = jnp.concatenate([jnp.concatenate([p[k] for p in u_core + u_rest], 0) for k in range(2)], 1)

    def part(dest):
        left = lax.dynamic_slice(a_all, (0, (dest >> 1) * rows), (8 * count, rows))
        right = lax.dynamic_slice(u_all, (0, (dest & 1) * cols), (8 * count, cols))
        return lax.dot_general(
            left, right, (((0,), (0,)), ((), ())), preferred_element_type=jnp.float32
        )

    g_sent = jnp.stack([part(y ^ far ^ near), part(y ^ near)])
    g_one = lax.ppermute(g_sent, "fsdp", y_pairs(0))
    g_two = lax.ppermute(part(y ^ far) + g_one[0], "fsdp", y_pairs(1))
    gradient = part(y) + g_one[1] + g_two

    fix_one = 1.0 - beta_one**STEP
    fix_two = 1.0 - beta_two**STEP
    params = inner_params[0, 0]
    moment_one = beta_one * first_moment[0, 0] + (1.0 - beta_one) * gradient
    moment_two = beta_two * second_moment[0, 0] + (1.0 - beta_two) * gradient * gradient
    update = (
        moment_one / fix_one / (jnp.sqrt(moment_two / fix_two) + adam_eps) + decay_rate * params
    )
    stepped = params - inner_rate * update

    slice_rows = rows // members
    parts = lax.all_to_all(
        stepped.reshape(members, slice_rows, cols), "replica", split_axis=0, concat_axis=0, tiled=True
    )
    pseudo = anchor[0] - jnp.sum(parts, axis=0) / members
    new_momentum = outer_mu * outer_momentum[0] + pseudo
    new_params = anchor[0] - outer_rate * (pseudo + outer_mu * new_momentum)
    gathered = lax.all_to_all(
        jnp.broadcast_to(new_params[None], (members, slice_rows, cols)),
        "replica",
        split_axis=0,
        concat_axis=0,
        tiled=True,
    ).reshape(rows, cols)
    return (gathered[None], new_momentum[None], moment_one[None, None], moment_two[None, None])


def solution(mesh):
    in_specs = (
        P("replica", "fsdp", None),
        P("replica", "fsdp", None),
        P("replica", "fsdp", None, None),
        P("replica", "fsdp", None, None),
        P("replica", "fsdp", None, None),
        P("fsdp", "replica", None),
        P("fsdp", "replica", None),
    )
    out_specs = (
        P("fsdp", None, None),
        P("fsdp", "replica", None),
        P("replica", "fsdp", None, None),
        P("replica", "fsdp", None, None),
    )
    return jax.shard_map(body, mesh=mesh, in_specs=in_specs, out_specs=out_specs, check_vma=False)
```

```python
import jax
import jax.numpy as jnp
from jax import lax
from jax.experimental import pallas as pl
from jax.sharding import PartitionSpec as P

STEP = 500


beta_one = 0.9
beta_two = 0.95
adam_eps = 1e-08
decay_rate = 0.1
inner_rate = 0.02
outer_rate = 0.7
outer_mu = 0.9

SIDE = 4
SHARDS = 32


def ring_partner(i, stage):
    return i ^ 1 if stage == 0 else i ^ 3


def place(i):
    return i // 8, i // 2 % SIDE, i % 2


def core_pairs():
    return [(i, i ^ 1) for i in range(SHARDS)]


def x_pairs(stage):
    pairs = []
    for i in range(SHARDS):
        x, y, c = place(i)
        pairs.append((i, ring_partner(x, stage ^ c) * 8 + y * 2 + c))
    return pairs


def y_pairs(stage):
    pairs = []
    for i in range(SHARDS):
        x, y, c = place(i)
        pairs.append((i, x * 8 + ring_partner(y, stage ^ c) * 2 + c))
    return pairs


def after(value, *others):
    others = [lax.slice(t, (0, 0), (16, 128)) for t in others]
    return pl.pallas_call(
        lambda *refs: None,
        out_shape=jax.ShapeDtypeStruct(value.shape, value.dtype),
        in_specs=[pl.BlockSpec(memory_space=pl.ANY)] * (1 + len(others)),
        out_specs=pl.BlockSpec(memory_space=pl.ANY),
        input_output_aliases={0: 0},
    )(value, *others)


def body(acts, upstream, inner_params, first_moment, second_moment, anchor, outer_momentum):
    members = lax.axis_size("replica")
    me = lax.axis_index("fsdp")
    x, y, c = me >> 3, (me >> 1) & 3, me & 1
    near, far = jnp.where(c == 0, 1, 3), jnp.where(c == 0, 3, 1)
    a = acts[0]
    u = upstream[0]
    count = a.shape[0]
    rows, cols = 256, 512

    halves = 2
    width = cols // halves

    def a_for(dest):
        return lax.dynamic_slice(a, (0, dest * 2 * rows), (count, 2 * rows))

    def u_for(core, j):
        return jnp.concatenate(
            [
                lax.dynamic_slice(u, (0, (k * 2 + core) * cols + j * width), (count, width))
                for k in range(2)
            ],
            1,
        )

    def pieces(t):
        return [t[i * count : (i + 1) * count] for i in range(t.shape[0] // count)]

    def gather_x(mine):
        one = lax.ppermute(mine, "fsdp", x_pairs(0))
        two = lax.ppermute(mine, "fsdp", x_pairs(1))
        return mine, one, two, lax.ppermute(one, "fsdp", x_pairs(1))

    swap = lax.ppermute(
        jnp.concatenate([u_for(1 - c, j) for j in range(halves)], 0), "fsdp", core_pairs()
    )
    a_one = lax.ppermute(jnp.concatenate([a_for(x ^ near), a_for(x ^ 2)], 0), "fsdp", x_pairs(0))
    a_one = after(a_one, swap)
    a_two = lax.ppermute(
        jnp.concatenate([a_for(x ^ far), a_one[count:]], 0), "fsdp", x_pairs(1)
    )
    mine = [
        jnp.concatenate([u_for(c, j), swap[j * count : (j + 1) * count]], 0) for j in range(halves)
    ]
    first = gather_x(mine[0])
    a_two = after(a_two, first[1])
    a_core = jnp.concatenate([a_for(x), a_one[:count], a_two], 0)
    a_other = lax.ppermute(a_core, "fsdp", core_pairs())
    own, other = pieces(a_core), pieces(a_other)
    a_chips = [jnp.concatenate([own[i], other[j]], 0) for i, j in enumerate((0, 2, 1, 3))]

    def chunk_sum(gathered):
        return sum(
            lax.dot_general(
                left, right, (((0,), (0,)), ((), ())), preferred_element_type=jnp.float32
            )
            for left, right in zip(a_chips, gathered)
        )

    def reduce_y(whole):
        def part(dest):
            return lax.dynamic_slice(
                whole, ((dest >> 1) * rows, (dest & 1) * width), (rows, width)
            )

        g_one = lax.ppermute(jnp.stack([part(y ^ 2), part(y ^ near)]), "fsdp", y_pairs(0))
        passed_on = part(y ^ far) + g_one[0]
        g_two = lax.ppermute(passed_on, "fsdp", y_pairs(1))
        return part(y) + g_one[1] + g_two, passed_on

    fix_one = 1.0 - beta_one**STEP
    fix_two = 1.0 - beta_two**STEP
    slice_rows = rows // members

    second = gather_x(after(mine[1], first[2], a_other))
    near_done, token = reduce_y(chunk_sum(first))
    far_done, _ = reduce_y(chunk_sum((*second[:3], after(second[3], token))))
    gradient = jnp.concatenate([near_done, far_done], 1)

    params = inner_params[0, 0]
    moment_one = beta_one * first_moment[0, 0] + (1.0 - beta_one) * gradient
    moment_two = beta_two * second_moment[0, 0] + (1.0 - beta_two) * gradient * gradient
    update = (
        moment_one / fix_one / (jnp.sqrt(moment_two / fix_two) + adam_eps) + decay_rate * params
    )
    stepped = params - inner_rate * update
    parts = lax.all_to_all(
        stepped.reshape(members, slice_rows, cols),
        "replica",
        split_axis=0,
        concat_axis=0,
        tiled=True,
    )
    total = jnp.sum(parts, axis=0)
    pseudo = anchor[0] - total / members
    new_momentum = outer_mu * outer_momentum[0] + pseudo
    new_params = anchor[0] - outer_rate * (pseudo + outer_mu * new_momentum)
    gathered = lax.all_to_all(
        jnp.broadcast_to(new_params[None], (members, slice_rows, cols)),
        "replica",
        split_axis=0,
        concat_axis=0,
        tiled=True,
    ).reshape(rows, cols)
    return (gathered[None], new_momentum[None], moment_one[None, None], moment_two[None, None])


def solution(mesh):
    in_specs = (
        P("replica", "fsdp", None),
        P("replica", "fsdp", None),
        P("replica", "fsdp", None, None),
        P("replica", "fsdp", None, None),
        P("replica", "fsdp", None, None),
        P("fsdp", "replica", None),
        P("fsdp", "replica", None),
    )
    out_specs = (
        P("fsdp", None, None),
        P("fsdp", "replica", None),
        P("replica", "fsdp", None, None),
        P("replica", "fsdp", None, None),
    )
    return jax.shard_map(body, mesh=mesh, in_specs=in_specs, out_specs=out_specs, check_vma=False)
```

```python
import jax
import jax.numpy as jnp
from jax import lax
from jax.experimental import pallas as pl
from jax.experimental.pallas import tpu as pltpu
from jax.sharding import PartitionSpec as P

STEP = 500


beta_one = 0.9
beta_two = 0.95
adam_eps = 1e-08
decay_rate = 0.1
inner_rate = 0.02
outer_rate = 0.7
outer_mu = 0.9

SIDE = 4
SHARDS = 32


def ring_partner(i, stage):
    return i ^ 1 if stage == 0 else i ^ 3


def place(i):
    return i // 8, i // 2 % SIDE, i % 2


def core_pairs():
    return [(i, i ^ 1) for i in range(SHARDS)]


def x_pairs(stage):
    pairs = []
    for i in range(SHARDS):
        x, y, c = place(i)
        pairs.append((i, ring_partner(x, stage ^ c) * 8 + y * 2 + c))
    return pairs


def y_pairs(stage):
    pairs = []
    for i in range(SHARDS):
        x, y, c = place(i)
        pairs.append((i, x * 8 + ring_partner(y, stage ^ c) * 2 + c))
    return pairs


def after(value, other):
    return pl.pallas_call(
        lambda *refs: None,
        out_shape=jax.ShapeDtypeStruct(value.shape, value.dtype),
        in_specs=[pl.BlockSpec(memory_space=pl.ANY), pl.BlockSpec(memory_space=pltpu.VMEM)],
        out_specs=pl.BlockSpec(memory_space=pl.ANY),
        input_output_aliases={0: 0},
        cost_estimate=pl.CostEstimate(flops=1 << 36, bytes_accessed=0, transcendentals=0),
    )(value, other)


def body(acts, upstream, inner_params, first_moment, second_moment, anchor, outer_momentum):
    members = lax.axis_size("replica")
    me = lax.axis_index("fsdp")
    x, y, c = me >> 3, (me >> 1) & 3, me & 1
    near, far = jnp.where(c == 0, 1, 3), jnp.where(c == 0, 3, 1)
    a = acts[0]
    u = upstream[0]
    count = a.shape[0]
    rows, cols = 256, 512

    halves = 2
    width = cols // halves

    def a_for(dest):
        return lax.dynamic_slice(a, (0, dest * 2 * rows), (count, 2 * rows))

    def u_for(j):
        at = [(k * 2 + core) * cols + j * width for core in range(2) for k in range(2)]
        parts = [u[:, i : i + width] for i in at]
        return jnp.concatenate(
            [jnp.concatenate(parts[:2], 1), jnp.concatenate(parts[2:], 1)], 0
        )

    def pieces(t):
        return [t[i * count : (i + 1) * count] for i in range(t.shape[0] // count)]

    u_zero = u_for(0)
    one = lax.ppermute(
        jnp.concatenate([a_for(x ^ near), u_zero, a_for(x ^ 2)], 0), "fsdp", x_pairs(0)
    )
    two = lax.ppermute(jnp.concatenate([u_zero, a_for(x ^ far)], 0), "fsdp", x_pairs(1))
    three = lax.ppermute(one[count:], "fsdp", x_pairs(1))
    a_chips = [a_for(x), one[:count], two[2 * count :], three[2 * count :]]
    zero = [u_zero, one[count : 3 * count], two[: 2 * count], three[: 2 * count]]

    u_one = after(u_for(1), one)
    next_one = lax.ppermute(u_one, "fsdp", x_pairs(0))
    next_two = lax.ppermute(after(u_one, three), "fsdp", x_pairs(1))
    next_three = lax.ppermute(after(next_one, three), "fsdp", x_pairs(1))

    def chunk_sum(gathered, behind=None):
        def half(core):
            return sum(
                lax.dot_general(
                    left,
                    lax.dynamic_slice(right, (core * count, 0), (count, cols)),
                    (((0,), (0,)), ((), ())),
                    preferred_element_type=jnp.float32,
                )
                for left, right in zip(a_chips, gathered)
            )

        arrived = lax.ppermute(half(1 - c), "fsdp", core_pairs())
        return half(c) + (arrived if behind is None else after(arrived, behind))

    def reduce_y(whole):
        def part(dest):
            return lax.dynamic_slice(
                whole, ((dest >> 1) * rows, (dest & 1) * width), (rows, width)
            )

        g_one = lax.ppermute(jnp.stack([part(y ^ 2), part(y ^ near)]), "fsdp", y_pairs(0))
        g_two = lax.ppermute(part(y ^ far) + g_one[0], "fsdp", y_pairs(1))
        return part(y) + g_one[1] + g_two, g_one

    fix_one = 1.0 - beta_one**STEP
    fix_two = 1.0 - beta_two**STEP
    slice_rows = rows // members

    sum_zero = chunk_sum(zero)
    done_zero, g_zero = reduce_y(sum_zero)
    next_three = after(next_three, sum_zero)
    done_one, _ = reduce_y(chunk_sum([u_one, next_one, next_two, next_three], g_zero))
    gradient = jnp.concatenate([done_zero, done_one], 1)

    params = inner_params[0, 0]
    moment_one = beta_one * first_moment[0, 0] + (1.0 - beta_one) * gradient
    moment_two = beta_two * second_moment[0, 0] + (1.0 - beta_two) * gradient * gradient
    update = (
        moment_one / fix_one / (jnp.sqrt(moment_two / fix_two) + adam_eps) + decay_rate * params
    )
    stepped = params - inner_rate * update
    parts = lax.all_to_all(
        stepped.reshape(members, slice_rows, cols),
        "replica",
        split_axis=0,
        concat_axis=0,
        tiled=True,
    )
    total = jnp.sum(parts, axis=0)
    pseudo = anchor[0] - total / members
    new_momentum = outer_mu * outer_momentum[0] + pseudo
    new_params = anchor[0] - outer_rate * (pseudo + outer_mu * new_momentum)
    gathered = lax.all_to_all(
        jnp.broadcast_to(new_params[None], (members, slice_rows, cols)),
        "replica",
        split_axis=0,
        concat_axis=0,
        tiled=True,
    ).reshape(rows, cols)
    return (gathered[None], new_momentum[None], moment_one[None, None], moment_two[None, None])


def solution(mesh):
    in_specs = (
        P("replica", "fsdp", None),
        P("replica", "fsdp", None),
        P("replica", "fsdp", None, None),
        P("replica", "fsdp", None, None),
        P("replica", "fsdp", None, None),
        P("fsdp", "replica", None),
        P("fsdp", "replica", None),
    )
    out_specs = (
        P("fsdp", None, None),
        P("fsdp", "replica", None),
        P("replica", "fsdp", None, None),
        P("replica", "fsdp", None, None),
    )
    return jax.shard_map(body, mesh=mesh, in_specs=in_specs, out_specs=out_specs, check_vma=False)
```

```python
import jax
import jax.numpy as jnp
from jax import lax
from jax.sharding import PartitionSpec as P

STEP = 500


beta_one = 0.9
beta_two = 0.95
adam_eps = 1e-08
decay_rate = 0.1
inner_rate = 0.02
outer_rate = 0.7
outer_mu = 0.9

SIDE = 4
SHARDS = 32


def ring_partner(i, stage):
    return i ^ 1 if stage == 0 else i ^ 3


def place(i):
    return i // 8, i // 2 % SIDE, i % 2


def core_pairs():
    return [(i, i ^ 1) for i in range(SHARDS)]


def x_pairs(stage):
    pairs = []
    for i in range(SHARDS):
        x, y, c = place(i)
        pairs.append((i, ring_partner(x, stage ^ c) * 8 + y * 2 + c))
    return pairs


def y_pairs(stage):
    pairs = []
    for i in range(SHARDS):
        x, y, c = place(i)
        pairs.append((i, x * 8 + ring_partner(y, stage ^ c) * 2 + c))
    return pairs


def body(acts, upstream, inner_params, first_moment, second_moment, anchor, outer_momentum):
    members = lax.axis_size("replica")
    me = lax.axis_index("fsdp")
    x, y, c = me >> 3, (me >> 1) & 3, me & 1
    near, far = jnp.where(c == 0, 1, 3), jnp.where(c == 0, 3, 1)
    a = acts[0]
    u = upstream[0]
    count = a.shape[0]
    rows, cols = 256, 512

    def a_for(dest):
        return lax.dynamic_slice(a, (0, dest * 2 * rows), (count, 2 * rows))

    def u_for(core):
        return [lax.dynamic_slice(u, (0, (k * 2 + core) * cols), (count, cols)) for k in range(2)]

    def pieces(t):
        return [t[i * count : (i + 1) * count] for i in range(t.shape[0] // count)]

    u_own = u_for(c)
    u_swap = lax.ppermute(jnp.concatenate(u_for(1 - c), 0), "fsdp", core_pairs())
    one = lax.ppermute(
        jnp.concatenate([a_for(x ^ near), *u_own, a_for(x ^ 2)], 0), "fsdp", x_pairs(0)
    )
    two = lax.ppermute(jnp.concatenate([a_for(x ^ far), *u_own], 0), "fsdp", x_pairs(1))
    one_swap = lax.ppermute(u_swap, "fsdp", x_pairs(0))
    two_swap = lax.ppermute(u_swap, "fsdp", x_pairs(1))
    three = lax.ppermute(one[count:], "fsdp", x_pairs(1))
    three_swap = lax.ppermute(one_swap, "fsdp", x_pairs(1))
    a_core = jnp.concatenate([a_for(x), one[:count], two[:count], three[2 * count :]], 0)
    a_other = lax.ppermute(a_core, "fsdp", core_pairs())
    other = pieces(a_other)
    a_all = jnp.concatenate([a_core, other[0], other[2], other[1], other[3]], 0)
    u_core = [u_own, pieces(one)[1:3], pieces(two)[1:], pieces(three)[:2]]
    u_rest = [pieces(u_swap), pieces(one_swap), pieces(two_swap), pieces(three_swap)]
    u_all = jnp.concatenate([jnp.concatenate([p[k] for p in u_core + u_rest], 0) for k in range(2)], 1)

    def part(dest):
        left = lax.dynamic_slice(a_all, (0, (dest >> 1) * rows), (8 * count, rows))
        right = lax.dynamic_slice(u_all, (0, (dest & 1) * cols), (8 * count, cols))
        return lax.dot_general(
            left, right, (((0,), (0,)), ((), ())), preferred_element_type=jnp.float32
        )

    g_far = lax.ppermute(part(y ^ 2), "fsdp", y_pairs(0))
    g_near = lax.ppermute(part(y ^ near), "fsdp", y_pairs(0))
    kept_far, kept = lax.optimization_barrier((part(y ^ far), part(y)))
    g_two = lax.ppermute(kept_far + g_far, "fsdp", y_pairs(1))
    gradient = kept + g_near + g_two

    fix_one = 1.0 - beta_one**STEP
    fix_two = 1.0 - beta_two**STEP
    params = inner_params[0, 0]
    moment_one = beta_one * first_moment[0, 0] + (1.0 - beta_one) * gradient
    moment_two = beta_two * second_moment[0, 0] + (1.0 - beta_two) * gradient * gradient
    update = (
        moment_one / fix_one / (jnp.sqrt(moment_two / fix_two) + adam_eps) + decay_rate * params
    )
    stepped = params - inner_rate * update

    slice_rows = rows // members
    parts = lax.all_to_all(
        stepped.reshape(members, slice_rows, cols), "replica", split_axis=0, concat_axis=0, tiled=True
    )
    pseudo = anchor[0] - jnp.sum(parts, axis=0) / members
    new_momentum = outer_mu * outer_momentum[0] + pseudo
    new_params = anchor[0] - outer_rate * (pseudo + outer_mu * new_momentum)
    gathered = lax.all_to_all(
        jnp.broadcast_to(new_params[None], (members, slice_rows, cols)),
        "replica",
        split_axis=0,
        concat_axis=0,
        tiled=True,
    ).reshape(rows, cols)
    return (gathered[None], new_momentum[None], moment_one[None, None], moment_two[None, None])


def solution(mesh):
    in_specs = (
        P("replica", "fsdp", None),
        P("replica", "fsdp", None),
        P("replica", "fsdp", None, None),
        P("replica", "fsdp", None, None),
        P("replica", "fsdp", None, None),
        P("fsdp", "replica", None),
        P("fsdp", "replica", None),
    )
    out_specs = (
        P("fsdp", None, None),
        P("fsdp", "replica", None),
        P("replica", "fsdp", None, None),
        P("replica", "fsdp", None, None),
    )
    return jax.shard_map(body, mesh=mesh, in_specs=in_specs, out_specs=out_specs, check_vma=False)
```

```python
import jax
import jax.numpy as jnp
from jax import lax
from jax.sharding import PartitionSpec as P

STEP = 500


beta_one = 0.9
beta_two = 0.95
adam_eps = 1e-08
decay_rate = 0.1
inner_rate = 0.02
outer_rate = 0.7
outer_mu = 0.9

SIDE = 4
SHARDS = 32


def ring_partner(i, stage):
    return i ^ 1 if stage == 0 else i ^ 3


def place(i):
    return i // 8, i // 2 % SIDE, i % 2


def core_pairs():
    return [(i, i ^ 1) for i in range(SHARDS)]


def x_pairs(stage):
    pairs = []
    for i in range(SHARDS):
        x, y, c = place(i)
        pairs.append((i, ring_partner(x, stage ^ c) * 8 + y * 2 + c))
    return pairs


def y_pairs(stage):
    pairs = []
    for i in range(SHARDS):
        x, y, c = place(i)
        pairs.append((i, x * 8 + ring_partner(y, stage ^ c) * 2 + c))
    return pairs


def body(acts, upstream, inner_params, first_moment, second_moment, anchor, outer_momentum):
    members = lax.axis_size("replica")
    me = lax.axis_index("fsdp")
    x, y, c = me >> 3, (me >> 1) & 3, me & 1
    near, far = jnp.where(c == 0, 1, 3), jnp.where(c == 0, 3, 1)
    a = acts[0]
    u = upstream[0]
    count = a.shape[0]
    rows, cols = 256, 512

    def a_for(dest):
        return lax.dynamic_slice(a, (0, dest * 2 * rows), (count, 2 * rows))

    def u_for(core):
        return [lax.dynamic_slice(u, (0, (k * 2 + core) * cols), (count, cols)) for k in range(2)]

    def pieces(t):
        return [t[i * count : (i + 1) * count] for i in range(t.shape[0] // count)]

    u_own = lax.optimization_barrier(u_for(c))
    u_swap = lax.ppermute(jnp.concatenate(u_for(1 - c), 0), "fsdp", core_pairs())
    one = lax.ppermute(
        jnp.concatenate([a_for(x ^ near), *u_own, a_for(x ^ 2)], 0), "fsdp", x_pairs(0)
    )
    two = lax.ppermute(jnp.concatenate([a_for(x ^ far), *u_own], 0), "fsdp", x_pairs(1))
    one_swap = lax.ppermute(u_swap, "fsdp", x_pairs(0))
    two_swap = lax.ppermute(u_swap, "fsdp", x_pairs(1))
    three = lax.ppermute(one[count:], "fsdp", x_pairs(1))
    three_swap = lax.ppermute(one_swap, "fsdp", x_pairs(1))
    a_core = jnp.concatenate([a_for(x), one[:count], two[:count], three[2 * count :]], 0)
    a_other = lax.ppermute(a_core, "fsdp", core_pairs())
    other = pieces(a_other)
    a_all = jnp.concatenate([a_core, other[0], other[2], other[1], other[3]], 0)
    u_core = [u_own, pieces(one)[1:3], pieces(two)[1:], pieces(three)[:2]]
    u_rest = [pieces(u_swap), pieces(one_swap), pieces(two_swap), pieces(three_swap)]
    u_all = jnp.concatenate([jnp.concatenate([p[k] for p in u_core + u_rest], 0) for k in range(2)], 1)

    def part(dest):
        left = lax.dynamic_slice(a_all, (0, (dest >> 1) * rows), (8 * count, rows))
        right = lax.dynamic_slice(u_all, (0, (dest & 1) * cols), (8 * count, cols))
        return lax.dot_general(
            left, right, (((0,), (0,)), ((), ())), preferred_element_type=jnp.float32
        )

    g_far = lax.ppermute(part(y ^ 2), "fsdp", y_pairs(0))
    g_near = lax.ppermute(part(y ^ near), "fsdp", y_pairs(0))
    kept_far, kept = lax.optimization_barrier((part(y ^ far), part(y)))
    g_two = lax.ppermute(kept_far + g_far, "fsdp", y_pairs(1))
    gradient = kept + g_near + g_two

    fix_one = 1.0 - beta_one**STEP
    fix_two = 1.0 - beta_two**STEP
    params = inner_params[0, 0]

    def moments(g, first, second):
        return (
            beta_one * first + (1.0 - beta_one) * g,
            beta_two * second + (1.0 - beta_two) * g * g,
        )

    moment_one, moment_two = moments(gradient, first_moment[0, 0], second_moment[0, 0])
    update = (
        moment_one / fix_one / (jnp.sqrt(moment_two / fix_two) + adam_eps) + decay_rate * params
    )
    moment_one, moment_two = moments(
        *lax.optimization_barrier((gradient, first_moment[0, 0], second_moment[0, 0]))
    )
    stepped = params - inner_rate * update

    slice_rows = rows // members
    parts = lax.all_to_all(
        stepped.reshape(members, slice_rows, cols), "replica", split_axis=0, concat_axis=0, tiled=True
    )
    def outer(mean, anchor, momentum):
        pseudo = anchor - mean
        momentum = outer_mu * momentum + pseudo
        return momentum, anchor - outer_rate * (pseudo + outer_mu * momentum)

    mean = jnp.sum(parts, axis=0) / members
    _, new_params = outer(mean, anchor[0], outer_momentum[0])
    new_momentum, _ = outer(*lax.optimization_barrier((mean, anchor[0], outer_momentum[0])))
    gathered = lax.all_to_all(
        jnp.broadcast_to(new_params[None], (members, slice_rows, cols)),
        "replica",
        split_axis=0,
        concat_axis=0,
        tiled=True,
    ).reshape(rows, cols)
    return (gathered[None], new_momentum[None], moment_one[None, None], moment_two[None, None])


def solution(mesh):
    in_specs = (
        P("replica", "fsdp", None),
        P("replica", "fsdp", None),
        P("replica", "fsdp", None, None),
        P("replica", "fsdp", None, None),
        P("replica", "fsdp", None, None),
        P("fsdp", "replica", None),
        P("fsdp", "replica", None),
    )
    out_specs = (
        P("fsdp", None, None),
        P("fsdp", "replica", None),
        P("replica", "fsdp", None, None),
        P("replica", "fsdp", None, None),
    )
    return jax.shard_map(body, mesh=mesh, in_specs=in_specs, out_specs=out_specs, check_vma=False)
```

```python
import jax
import jax.numpy as jnp
from jax import lax
from jax.sharding import PartitionSpec as P

STEP = 500


beta_one = 0.9
beta_two = 0.95
adam_eps = 1e-08
decay_rate = 0.1
inner_rate = 0.02
outer_rate = 0.7
outer_mu = 0.9

SIDE = 4
SHARDS = 32


def ring_partner(i, stage):
    return i ^ 1 if stage == 0 else i ^ 3


def place(i):
    return i // 8, i // 2 % SIDE, i % 2


def core_pairs():
    return [(i, i ^ 1) for i in range(SHARDS)]


def x_pairs(stage):
    pairs = []
    for i in range(SHARDS):
        x, y, c = place(i)
        pairs.append((i, ring_partner(x, stage ^ c) * 8 + y * 2 + c))
    return pairs


def y_pairs(stage):
    pairs = []
    for i in range(SHARDS):
        x, y, c = place(i)
        pairs.append((i, x * 8 + ring_partner(y, stage ^ c) * 2 + c))
    return pairs


def after(value, other):
    return jnp.where(other == other, value, jnp.zeros_like(value))


def body(acts, upstream, inner_params, first_moment, second_moment, anchor, outer_momentum):
    members = lax.axis_size("replica")
    me = lax.axis_index("fsdp")
    x, y, c = me >> 3, (me >> 1) & 3, me & 1
    near, far = jnp.where(c == 0, 1, 3), jnp.where(c == 0, 3, 1)
    a = acts[0]
    u = upstream[0]
    count = a.shape[0]
    rows, cols = 256, 512

    def a_for(dest):
        return lax.dynamic_slice(a, (0, dest * 2 * rows), (count, 2 * rows))

    first = y & 1

    def u_for(core):
        return [
            lax.dynamic_slice(u, (0, (k * 2 + core) * cols), (count, cols))
            for k in (first, 1 - first)
        ]

    def pieces(t):
        return [t[i * count : (i + 1) * count] for i in range(t.shape[0] // count)]

    u_own = lax.optimization_barrier(u_for(c))
    u_swap = lax.ppermute(jnp.concatenate(u_for(1 - c), 0), "fsdp", core_pairs())
    one = lax.ppermute(
        jnp.concatenate([a_for(x ^ near), *u_own, a_for(x ^ 2)], 0), "fsdp", x_pairs(0)
    )
    two = lax.ppermute(jnp.concatenate([a_for(x ^ far), *u_own], 0), "fsdp", x_pairs(1))
    one_swap = lax.ppermute(u_swap, "fsdp", x_pairs(0))
    two_swap = pieces(lax.ppermute(u_swap, "fsdp", x_pairs(1)))
    three = lax.ppermute(one[count:], "fsdp", x_pairs(1))
    three_swap = pieces(lax.ppermute(one_swap, "fsdp", x_pairs(1)))
    a_core = jnp.concatenate([a_for(x), one[:count], two[:count], three[2 * count :]], 0)
    a_other = lax.ppermute(a_core, "fsdp", core_pairs())
    other = pieces(a_other)
    a_all = jnp.concatenate([a_core, other[0], other[2], other[1], other[3]], 0)
    u_core = [u_own, pieces(one)[1:3], pieces(two)[1:], pieces(three)[:2]]
    u_rest = [pieces(u_swap), pieces(one_swap), two_swap, three_swap]
    u_all = [jnp.concatenate([p[k] for p in u_core + u_rest], 0) for k in range(2)]

    def part(dest, side):
        left = lax.dynamic_slice(a_all, (0, (dest >> 1) * rows), (8 * count, rows))
        return lax.dot_general(
            left, u_all[side], (((0,), (0,)), ((), ())), preferred_element_type=jnp.float32
        )

    sent_far = part(y ^ 2, 0)
    g_far = lax.ppermute(sent_far, "fsdp", y_pairs(0))
    g_near = lax.ppermute(after(part(y ^ near, 1), sent_far), "fsdp", y_pairs(0))
    kept_far, kept = lax.optimization_barrier((part(y ^ far, 1), part(y, 0)))
    g_two = lax.ppermute(kept_far + g_far, "fsdp", y_pairs(1))
    gradient = kept + g_near + g_two

    fix_one = 1.0 - beta_one**STEP
    fix_two = 1.0 - beta_two**STEP
    params = inner_params[0, 0]

    def moments(g, first, second):
        return (
            beta_one * first + (1.0 - beta_one) * g,
            beta_two * second + (1.0 - beta_two) * g * g,
        )

    moment_one, moment_two = moments(gradient, first_moment[0, 0], second_moment[0, 0])
    update = (
        moment_one / fix_one / (jnp.sqrt(moment_two / fix_two) + adam_eps) + decay_rate * params
    )
    moment_one, moment_two = moments(
        *lax.optimization_barrier((gradient, first_moment[0, 0], second_moment[0, 0]))
    )
    stepped = params - inner_rate * update

    slice_rows = rows // members
    parts = lax.all_to_all(
        stepped.reshape(members, slice_rows, cols), "replica", split_axis=0, concat_axis=0, tiled=True
    )
    def outer(mean, anchor, momentum):
        pseudo = anchor - mean
        momentum = outer_mu * momentum + pseudo
        return momentum, anchor - outer_rate * (pseudo + outer_mu * momentum)

    mean = jnp.sum(parts, axis=0) / members
    _, new_params = outer(mean, anchor[0], outer_momentum[0])
    new_momentum, _ = outer(*lax.optimization_barrier((mean, anchor[0], outer_momentum[0])))
    gathered = lax.all_to_all(
        jnp.broadcast_to(new_params[None], (members, slice_rows, cols)),
        "replica",
        split_axis=0,
        concat_axis=0,
        tiled=True,
    ).reshape(rows, cols)
    return (gathered[None], new_momentum[None], moment_one[None, None], moment_two[None, None])


def solution(mesh):
    in_specs = (
        P("replica", "fsdp", None),
        P("replica", "fsdp", None),
        P("replica", "fsdp", None, None),
        P("replica", "fsdp", None, None),
        P("replica", "fsdp", None, None),
        P("fsdp", "replica", None),
        P("fsdp", "replica", None),
    )
    out_specs = (
        P("fsdp", None, None),
        P("fsdp", "replica", None),
        P("replica", "fsdp", None, None),
        P("replica", "fsdp", None, None),
    )
    return jax.shard_map(body, mesh=mesh, in_specs=in_specs, out_specs=out_specs, check_vma=False)
```

```python
import jax
import jax.numpy as jnp
from jax import lax
from jax.sharding import PartitionSpec as P

STEP = 500


beta_one = 0.9
beta_two = 0.95
adam_eps = 1e-08
decay_rate = 0.1
inner_rate = 0.02
outer_rate = 0.7
outer_mu = 0.9

SIDE = 4
SHARDS = 32


def ring_partner(i, stage):
    return i ^ 1 if stage == 0 else i ^ 3


def place(i):
    return i // 8, i // 2 % SIDE, i % 2


def core_pairs():
    return [(i, i ^ 1) for i in range(SHARDS)]


def x_pairs(stage):
    pairs = []
    for i in range(SHARDS):
        x, y, c = place(i)
        pairs.append((i, ring_partner(x, stage ^ c) * 8 + y * 2 + c))
    return pairs


def y_pairs(stage):
    pairs = []
    for i in range(SHARDS):
        x, y, c = place(i)
        pairs.append((i, x * 8 + ring_partner(y, stage ^ c) * 2 + c))
    return pairs


def after(value, other):
    return jnp.where(other == other, value, jnp.zeros_like(value))


def body(acts, upstream, inner_params, first_moment, second_moment, anchor, outer_momentum):
    members = lax.axis_size("replica")
    me = lax.axis_index("fsdp")
    x, y, c = me >> 3, (me >> 1) & 3, me & 1
    near, far = jnp.where(c == 0, 1, 3), jnp.where(c == 0, 3, 1)
    a = acts[0]
    u = upstream[0]
    count = a.shape[0]
    rows, cols = 256, 512

    def a_for(dest):
        return lax.dynamic_slice(a, (0, dest * 2 * rows), (count, 2 * rows))

    first = y & 1

    def u_for(core):
        return [
            lax.dynamic_slice(u, (0, (k * 2 + core) * cols), (count, cols))
            for k in (first, 1 - first)
        ]

    def pieces(t):
        return [t[i * count : (i + 1) * count] for i in range(t.shape[0] // count)]

    u_own = lax.optimization_barrier(u_for(c))
    u_swap = lax.ppermute(jnp.concatenate(u_for(1 - c), 0), "fsdp", core_pairs())
    one = lax.ppermute(
        jnp.concatenate([a_for(x ^ near), *u_own, a_for(x ^ 2)], 0), "fsdp", x_pairs(0)
    )
    two = lax.ppermute(jnp.concatenate([a_for(x ^ far), *u_own], 0), "fsdp", x_pairs(1))
    one_swap = lax.ppermute(u_swap, "fsdp", x_pairs(0))
    two_swap = pieces(lax.ppermute(u_swap, "fsdp", x_pairs(1)))
    three = lax.ppermute(one[count:], "fsdp", x_pairs(1))
    three_swap = pieces(lax.ppermute(one_swap, "fsdp", x_pairs(1)))
    a_core = jnp.concatenate([a_for(x), one[:count], two[:count], three[2 * count :]], 0)
    a_other = lax.ppermute(a_core, "fsdp", core_pairs())
    other = pieces(a_other)
    a_all = jnp.concatenate([a_core, other[0], other[2], other[1], other[3]], 0)
    u_core = [u_own, pieces(one)[1:3], pieces(two)[1:], pieces(three)[:2]]
    u_rest = [pieces(u_swap), pieces(one_swap), two_swap, three_swap]
    u_all = [jnp.concatenate([p[k] for p in u_core + u_rest], 0) for k in range(2)]

    def part(dest, side):
        left = lax.dynamic_slice(a_all, (0, (dest >> 1) * rows), (8 * count, rows))
        return lax.dot_general(
            left, u_all[side], (((0,), (0,)), ((), ())), preferred_element_type=jnp.float32
        )

    sent_far = part(y ^ 2, 0)
    g_far = lax.ppermute(sent_far, "fsdp", y_pairs(0))
    g_near = lax.ppermute(after(part(y ^ near, 1), sent_far), "fsdp", y_pairs(0))
    kept_far, kept = lax.optimization_barrier((part(y ^ far, 1), part(y, 0)))
    g_two = lax.ppermute(kept_far + g_far, "fsdp", y_pairs(1))
    gradient = kept + g_near + g_two

    fix_one = 1.0 - beta_one**STEP
    fix_two = 1.0 - beta_two**STEP
    params = inner_params[0, 0]

    def moments(g, first, second):
        return (
            beta_one * first + (1.0 - beta_one) * g,
            beta_two * second + (1.0 - beta_two) * g * g,
        )

    moment_one, moment_two = moments(gradient, first_moment[0, 0], second_moment[0, 0])
    update = (
        moment_one / fix_one / (jnp.sqrt(moment_two / fix_two) + adam_eps) + decay_rate * params
    )
    moment_one, moment_two = moments(
        *lax.optimization_barrier((gradient, first_moment[0, 0], second_moment[0, 0]))
    )
    stepped = params - inner_rate * update

    slice_rows = rows // members
    parts = lax.all_to_all(
        stepped.reshape(members, slice_rows, cols), "replica", split_axis=0, concat_axis=0, tiled=True
    )
    def outer(mean, anchor, momentum):
        pseudo = anchor - mean
        momentum = outer_mu * momentum + pseudo
        return momentum, anchor - outer_rate * (pseudo + outer_mu * momentum)

    mean = jnp.sum(parts, axis=0) / members
    copies = (members, slice_rows, cols)
    _, new_params = outer(
        *(jnp.broadcast_to(t, copies) for t in (mean, anchor[0], outer_momentum[0]))
    )
    new_momentum, _ = outer(*lax.optimization_barrier((mean, anchor[0], outer_momentum[0])))
    gathered = lax.all_to_all(
        new_params,
        "replica",
        split_axis=0,
        concat_axis=0,
        tiled=True,
    ).reshape(rows, cols)
    return (gathered[None], new_momentum[None], moment_one[None, None], moment_two[None, None])


def solution(mesh):
    in_specs = (
        P("replica", "fsdp", None),
        P("replica", "fsdp", None),
        P("replica", "fsdp", None, None),
        P("replica", "fsdp", None, None),
        P("replica", "fsdp", None, None),
        P("fsdp", "replica", None),
        P("fsdp", "replica", None),
    )
    out_specs = (
        P("fsdp", None, None),
        P("fsdp", "replica", None),
        P("replica", "fsdp", None, None),
        P("replica", "fsdp", None, None),
    )
    return jax.shard_map(body, mesh=mesh, in_specs=in_specs, out_specs=out_specs, check_vma=False)
```

```python
import jax
import jax.numpy as jnp
from jax import lax
from jax.sharding import PartitionSpec as P

STEP = 500


beta_one = 0.9
beta_two = 0.95
adam_eps = 1e-08
decay_rate = 0.1
inner_rate = 0.02
outer_rate = 0.7
outer_mu = 0.9

SIDE = 4
SHARDS = 32


def ring_partner(i, stage):
    return i ^ 1 if stage == 0 else i ^ 3


def place(i):
    return i // 8, i // 2 % SIDE, i % 2


def core_pairs():
    return [(i, i ^ 1) for i in range(SHARDS)]


def x_pairs(stage):
    pairs = []
    for i in range(SHARDS):
        x, y, c = place(i)
        pairs.append((i, ring_partner(x, stage ^ c) * 8 + y * 2 + c))
    return pairs


def y_pairs(stage):
    pairs = []
    for i in range(SHARDS):
        x, y, c = place(i)
        pairs.append((i, x * 8 + ring_partner(y, stage ^ c) * 2 + c))
    return pairs


def after(value, other):
    return jnp.where(other == other, value, jnp.zeros_like(value))


def body(acts, upstream, inner_params, first_moment, second_moment, anchor, outer_momentum):
    members = lax.axis_size("replica")
    me = lax.axis_index("fsdp")
    x, y, c = me >> 3, (me >> 1) & 3, me & 1
    near, far = jnp.where(c == 0, 1, 3), jnp.where(c == 0, 3, 1)
    a = acts[0]
    u = upstream[0]
    count = a.shape[0]
    rows, cols = 256, 512

    def a_for(dest):
        return lax.dynamic_slice(a, (0, dest * 2 * rows), (count, 2 * rows))

    first = y & 1

    def u_for(core):
        return [
            lax.dynamic_slice(u, (0, (k * 2 + core) * cols), (count, cols))
            for k in (first, 1 - first)
        ]

    def pieces(t):
        return [t[i * count : (i + 1) * count] for i in range(t.shape[0] // count)]

    u_own = lax.optimization_barrier(u_for(c))
    u_swap = lax.ppermute(jnp.concatenate(u_for(1 - c), 0), "fsdp", core_pairs())
    one = lax.ppermute(
        jnp.concatenate([a_for(x ^ near), *u_own, a_for(x ^ 2)], 0), "fsdp", x_pairs(0)
    )
    two = lax.ppermute(jnp.concatenate([a_for(x ^ far), *u_own], 0), "fsdp", x_pairs(1))
    one_swap = lax.ppermute(u_swap, "fsdp", x_pairs(0))
    two_swap = pieces(lax.ppermute(u_swap, "fsdp", x_pairs(1)))
    three = lax.ppermute(one[count:], "fsdp", x_pairs(1))
    three_swap = pieces(lax.ppermute(one_swap, "fsdp", x_pairs(1)))
    a_core = jnp.concatenate([a_for(x), one[:count], two[:count], three[2 * count :]], 0)
    a_other = lax.ppermute(a_core, "fsdp", core_pairs())
    other = pieces(a_other)
    a_all = jnp.concatenate([a_core, other[0], other[2], other[1], other[3]], 0)
    u_core = [u_own, pieces(one)[1:3], pieces(two)[1:], pieces(three)[:2]]
    u_rest = [pieces(u_swap), pieces(one_swap), two_swap, three_swap]
    u_all = [jnp.concatenate([p[k] for p in u_core + u_rest], 0) for k in range(2)]

    def part(dest, side):
        left = lax.dynamic_slice(a_all, (0, (dest >> 1) * rows), (8 * count, rows))
        return lax.dot_general(
            left, u_all[side], (((0,), (0,)), ((), ())), preferred_element_type=jnp.float32
        )

    sent_far = part(y ^ 2, 0)
    g_far = lax.ppermute(sent_far, "fsdp", y_pairs(0))
    g_near = lax.ppermute(after(part(y ^ near, 1), sent_far), "fsdp", y_pairs(0))
    kept_far, kept = lax.optimization_barrier((part(y ^ far, 1), part(y, 0)))
    g_two = lax.ppermute(kept_far + g_far, "fsdp", y_pairs(1))
    gradient = kept + g_near + g_two

    fix_one = 1.0 - beta_one**STEP
    fix_two = 1.0 - beta_two**STEP
    params = inner_params[0, 0]

    def moments(g, first, second):
        return (
            beta_one * first + (1.0 - beta_one) * g,
            beta_two * second + (1.0 - beta_two) * g * g,
        )

    moment_one, moment_two = moments(gradient, first_moment[0, 0], second_moment[0, 0])
    update = (
        moment_one / fix_one / (jnp.sqrt(moment_two / fix_two) + adam_eps) + decay_rate * params
    )
    moment_one, moment_two = moments(
        *lax.optimization_barrier((gradient, first_moment[0, 0], second_moment[0, 0]))
    )
    stepped = params - inner_rate * update

    slice_rows = rows // members
    parts = lax.all_to_all(
        stepped.reshape(members, slice_rows, cols), "replica", split_axis=0, concat_axis=0, tiled=True
    )
    def outer(total, anchor, momentum):
        pseudo = anchor - total / members
        momentum = outer_mu * momentum + pseudo
        return momentum, anchor - outer_rate * (pseudo + outer_mu * momentum)

    total = jnp.sum(parts, axis=0)
    copies = (members, slice_rows, cols)
    _, new_params = outer(
        *(jnp.broadcast_to(t, copies) for t in (total, anchor[0], outer_momentum[0]))
    )
    new_momentum, _ = outer(*lax.optimization_barrier((total, anchor[0], outer_momentum[0])))
    gathered = lax.all_to_all(
        new_params,
        "replica",
        split_axis=0,
        concat_axis=0,
        tiled=True,
    ).reshape(rows, cols)
    return (gathered[None], new_momentum[None], moment_one[None, None], moment_two[None, None])


def solution(mesh):
    in_specs = (
        P("replica", "fsdp", None),
        P("replica", "fsdp", None),
        P("replica", "fsdp", None, None),
        P("replica", "fsdp", None, None),
        P("replica", "fsdp", None, None),
        P("fsdp", "replica", None),
        P("fsdp", "replica", None),
    )
    out_specs = (
        P("fsdp", None, None),
        P("fsdp", "replica", None),
        P("replica", "fsdp", None, None),
        P("replica", "fsdp", None, None),
    )
    return jax.shard_map(body, mesh=mesh, in_specs=in_specs, out_specs=out_specs, check_vma=False)
```
